256 devices in a mesh: seq: 64 (over z, y, core), mdl: 4 (over x).
Axes of the slice: x: 4, y: 4, z: 8, core: 2. Of those that a mesh axis runs over, the one named last changes fastest.
Arguments:
- tokens: bfloat16 [65536, 4096], P(('seq', 'mdl')), may hold values from -32 to 32
- w_query: bfloat16 [4096, 2048], P('mdl'), may hold values from -0.09375 to 0.09375
- key_weight: bfloat16 [4096, 512], P('mdl'), may hold values from -0.09375 to 0.09375
- value_weight: bfloat16 [4096, 512], P('mdl'), may hold values from -0.09375 to 0.09375
- block_list: int32 [256, 8], P('seq'), may hold values from -1 to 254, as said below
Outputs:
- attended: bfloat16 [65536, 2048], P('seq', 'mdl')
The draws below stay inside these ranges and needn't reach their ends.
Inputs may be any that keep to these rules, and one draw needn't show every extreme that they name: Row b of block_list, with e = b // 4: its first entry is 0 (the sink block) for b >= 1 and -1 for b = 0; its second is b - 1 for b >= 2 and -1 otherwise; every other entry is -1 or a block j >= 1 with e - 31 <= j // 4 <= e - 2, the named blocks of a row distinct. Over the rows b with b // 4 = e, the blocks j >= 1 named with j // 4 = s number at most one for every s other than e.
All inputs are finite; a program needn't handle non-finite values.
Results may differ from the reference program's by a relative error of at most 0.035.
The reference program's roundings to bfloat16 on the way count: a program that leaves them out, or rounds other values in their place, can miss the bound.
Values may be sent and summed in bfloat16 or wider, within the bound.
No kernel may reach another device: no remote copies, remote signals or barrier semaphores. Data moves between devices by JAX's collectives and lax.ppermute only.
A program may use at most 192 MiB of HBM per device.

```python
import jax
import jax.numpy as jnp
from jax import lax

MODEL_WIDTH = 4096
HEAD_SIZE = 128
QUERY_HEADS = 16
KEY_VALUE_HEADS = 4
BLOCK_TOKENS_SIZE = 256
LIST = 8
TOKENS = 65536
NBD = 4
BLOCK_COUNT = 256
SPAN = 32


def draw_tokens(key, part):
    values = jax.random.truncated_normal(key, -6.0, 6.0, (TOKENS, MODEL_WIDTH), jnp.float32)
    return values.astype(jnp.bfloat16)


def draw_block_list(key, part):
    devices = BLOCK_COUNT // NBD
    width = max(SPAN - 2, LIST - 2)
    menu_key, nonzero_key, order_key = jax.random.split(key, 3)
    blocks = jnp.arange(BLOCK_COUNT, dtype=jnp.int32)[:, None]
    owner = blocks // NBD
    distance = jnp.arange(2, width + 2, dtype=jnp.int32)[None, :]
    source = owner - distance
    any_pick = jax.random.randint(menu_key, (devices, width), 0, NBD, dtype=jnp.int32)
    nonzero_pick = jax.random.randint(nonzero_key, (devices, width), 1, NBD, dtype=jnp.int32)
    owner_index = owner[:, 0]
    picks = jnp.where(source == 0, nonzero_pick[owner_index], any_pick[owner_index])
    valid = (source >= 0) & (distance <= SPAN - 1)
    ranks = jax.random.randint(order_key, (BLOCK_COUNT, width), 0, 1048576, dtype=jnp.int32)
    scores = ranks * width + (distance - 2)
    scores = jnp.where(valid, scores, 1073741824)
    order = jnp.argsort(scores, axis=1, stable=True)[:, :LIST - 2]
    chosen_source = jnp.take_along_axis(jnp.broadcast_to(source, (BLOCK_COUNT, width)), order, axis=1)
    chosen_pick = jnp.take_along_axis(picks, order, axis=1)
    chosen_valid = jnp.take_along_axis(jnp.broadcast_to(valid, (BLOCK_COUNT, width)), order, axis=1)
    entries = jnp.where(chosen_valid, chosen_source * NBD + chosen_pick, -1)
    sink = jnp.where(blocks >= 1, 0, -1)
    previous = jnp.where(blocks >= 2, blocks - 1, -1)
    return jnp.concatenate([sink, previous, entries], axis=1).astype(jnp.int32)


def block_scale(key, extent, pieces, smallest, top_value):
    factor_of, own = 1.0, jax.random.fold_in(key, 6)
    for axis_at, blocks in pieces:
        draws = jnp.exp(jax.random.uniform(jax.random.fold_in(own, axis_at), (blocks,), jnp.float32, smallest / len(pieces), top_value / len(pieces)))
        factor_of = factor_of * jnp.repeat(draws, extent[axis_at] // blocks).reshape([-1 if axis == axis_at else 1 for axis in range(len(extent))])
    return factor_of


def bell_draw(key, shape, deviation, reach, pieces=(), held_as=jnp.bfloat16):
    level = block_scale(key, shape, pieces, -0.22, 0.18) if pieces else 1.0
    drawn = jax.random.normal(key, shape, jnp.float32) * deviation * level
    return jnp.minimum(jnp.maximum(drawn, -reach), reach).astype(held_as)


def setup_inputs(seed: int = 0) -> dict:
    key_list = jax.random.split(jax.random.key(seed), 6)
    return {
        "tokens": draw_tokens(jax.random.fold_in(key_list[5], 71), 0),
        "w_query": bell_draw(key_list[1], (MODEL_WIDTH, QUERY_HEADS * HEAD_SIZE), MODEL_WIDTH ** -0.5, 0.09375, ((0, 4),)),
        "key_weight": bell_draw(key_list[2], (MODEL_WIDTH, KEY_VALUE_HEADS * HEAD_SIZE), MODEL_WIDTH ** -0.5, 0.09375, ((0, 4),)),
        "value_weight": bell_draw(key_list[3], (MODEL_WIDTH, KEY_VALUE_HEADS * HEAD_SIZE), MODEL_WIDTH ** -0.5, 0.09375, ((0, 4),)),
        "block_list": draw_block_list(jax.random.fold_in(key_list[5], 71), 0),
    }


THETA = 1000000.0


def apply_rotary(values, token_positions, heads):
    rows = values.shape[0]
    head_dim = values.shape[1] // heads
    half = head_dim // 2
    shaped = values.reshape(rows, heads, head_dim)
    freq = THETA ** (-jnp.arange(half, dtype=jnp.float32) / half)
    angle = token_positions.astype(jnp.float32)[:, None] * freq[None, :]
    cosine = jnp.cos(angle)[:, None, :]
    sine = jnp.sin(angle)[:, None, :]
    first = shaped[..., :half]
    second = shaped[..., half:]
    turned = jnp.concatenate([first * cosine - second * sine, second * cosine + first * sine], axis=-1)
    return turned.reshape(rows, heads * head_dim)


def reference(tokens, w_query, key_weight, value_weight, block_list):
    token_positions = jnp.arange(TOKENS, dtype=jnp.int32)
    query_matrix = apply_rotary(jnp.dot(tokens, w_query, preferred_element_type=jnp.float32), token_positions, QUERY_HEADS).astype(jnp.bfloat16)
    key = apply_rotary(jnp.dot(tokens, key_weight, preferred_element_type=jnp.float32), token_positions, KEY_VALUE_HEADS).astype(jnp.bfloat16)
    value_matrix = jnp.dot(tokens, value_weight, preferred_element_type=jnp.float32).astype(jnp.bfloat16)
    head_group = QUERY_HEADS // KEY_VALUE_HEADS
    blocked_queries = query_matrix.reshape(BLOCK_COUNT, BLOCK_TOKENS_SIZE, KEY_VALUE_HEADS, head_group, HEAD_SIZE)
    blocked_keys = key.reshape(BLOCK_COUNT, BLOCK_TOKENS_SIZE, KEY_VALUE_HEADS, HEAD_SIZE)
    blocked_values = value_matrix.reshape(BLOCK_COUNT, BLOCK_TOKENS_SIZE, KEY_VALUE_HEADS, HEAD_SIZE)
    causal = jnp.arange(BLOCK_TOKENS_SIZE)[:, None] >= jnp.arange(BLOCK_TOKENS_SIZE)[None, :]
    scale = 1.0 / (HEAD_SIZE ** 0.5)

    def one_block(block):
        row = block_list[block]
        valid = row >= 0
        index = jnp.maximum(row, 0).astype(jnp.int32)
        keys = jnp.concatenate([blocked_keys[index], blocked_keys[block][None]], axis=0).astype(jnp.float32)
        values = jnp.concatenate([blocked_values[index], blocked_values[block][None]], axis=0).astype(jnp.float32)
        listed = jnp.broadcast_to(valid[None, :, None], (BLOCK_TOKENS_SIZE, LIST, BLOCK_TOKENS_SIZE))
        mask = jnp.concatenate([listed, causal[:, None, :]], axis=1)
        queries = blocked_queries[block].astype(jnp.float32)
        scores = jnp.einsum("tkgd,lukd->kgtlu", queries, keys) * scale
        scores = jnp.where(mask[None, None], scores, -jnp.inf)
        top = jnp.max(scores, axis=(-2, -1), keepdims=True)
        weights = jnp.exp(scores - top)
        total = jnp.sum(weights, axis=(-2, -1))
        rounded = weights.astype(jnp.bfloat16).astype(jnp.float32)
        summed = jnp.einsum("kgtlu,lukd->tkgd", rounded, values)
        result = summed / jnp.transpose(total, (2, 0, 1))[..., None]
        return result.reshape(BLOCK_TOKENS_SIZE, QUERY_HEADS * HEAD_SIZE).astype(jnp.bfloat16)

    outputs = lax.map(one_block, jnp.arange(BLOCK_COUNT, dtype=jnp.int32))
    return outputs.reshape(TOKENS, QUERY_HEADS * HEAD_SIZE)
```

```python
import functools

import jax
import jax.numpy as jnp
from jax import lax
from jax.experimental import pallas as pl
from jax.experimental.pallas import tpu as pltpu
from jax.sharding import PartitionSpec as P

HEAD_SIZE = 128
BLOCK = 256
THETA = 1000000.0
CORES = 2
YS = 4
ROW = CORES * YS
HOPS = 5
MODELS = 4
FAR = HOPS * YS * CORES
VM = pl.BlockSpec(memory_space=pltpu.VMEM)
SM = pl.BlockSpec(memory_space=pltpu.SMEM)
HBM = pl.BlockSpec(memory_space=pltpu.HBM)
BF = jnp.bfloat16
F32 = jnp.float32


COST = pl.CostEstimate(flops=1, bytes_accessed=1, transcendentals=0)


def params(mib):
    return pltpu.CompilerParams(vmem_limit_bytes=mib * 2**20)


def along_x(value, steps):
    return lax.ppermute(value, "mdl", [(i, (i + steps) % MODELS) for i in range(MODELS)])


def along_z(value, steps):
    count = lax.axis_size("seq")
    return lax.ppermute(value, "seq", [(i, i + ROW * steps) for i in range(count - ROW * steps)])


def along_rows(value, rows, steps):
    pairs = [(i * ROW + j, (i + steps) * ROW + j) for i in rows for j in range(ROW)]
    return lax.ppermute(value, "seq", pairs)


def exchange_y(value):
    count = lax.axis_size("seq")
    groups = [
        [first + y * CORES + c for y in range(YS)] for first in range(0, count, ROW) for c in range(CORES)
    ]
    return lax.all_to_all(value, "seq", split_axis=0, concat_axis=0, axis_index_groups=groups)


def other_core(value):
    count = lax.axis_size("seq")
    return lax.ppermute(value, "seq", [(i, i ^ 1) for i in range(count)])


def columns_of(rank_ref, ahead, width):
    return pl.ds(pl.multiple_of(((rank_ref[0] + ahead) & (MODELS - 1)) * width, width), width)


def split_kernel(aheads, rank_ref, tokens, *refs):
    outs, sems = refs[:-1], refs[-1]
    width = outs[0].shape[1]
    copies = [
        pltpu.make_async_copy(tokens.at[:, columns_of(rank_ref, ahead, width)], outs[i], sems.at[i])
        for i, ahead in enumerate(aheads)
    ]
    for copy in copies:
        copy.start()
    for copy in copies:
        copy.wait()


def split(aheads, rank, tokens):
    shape = jax.ShapeDtypeStruct((tokens.shape[0], tokens.shape[1] // MODELS), BF)
    return pl.pallas_call(
        functools.partial(split_kernel, aheads),
        in_specs=[SM, HBM],
        out_specs=[VM] * len(aheads),
        out_shape=[shape] * len(aheads),
        scratch_shapes=[pltpu.SemaphoreType.DMA((len(aheads),))],
        compiler_params=params(4),
        cost_estimate=COST,
        name="split_columns",
    )(rank, pltpu.with_memory_space_constraint(tokens, pltpu.HBM))


def join_weights_kernel(wk, wv, out):
    for head in range(MODELS):
        column = slice(head * HEAD_SIZE, (head + 1) * HEAD_SIZE)
        out[head, :, :HEAD_SIZE] = wk[:, column]
        out[head, :, HEAD_SIZE:] = wv[:, column]


def join_weights(key_weight, value_weight):
    return pl.pallas_call(
        join_weights_kernel,
        in_specs=[VM] * 2,
        out_specs=VM,
        out_shape=jax.ShapeDtypeStruct((MODELS, key_weight.shape[0], 2 * HEAD_SIZE), BF),
        compiler_params=params(4),
        cost_estimate=COST,
        name="join_weights",
    )(key_weight, value_weight)


def kv_parts_kernel(aheads, rank_ref, t0, t1, t2, t3, w, *outs):
    rank = rank_ref[0]
    rows = t0.shape[0]
    for ahead, out in zip(aheads, outs):
        head = (rank + ahead) & (MODELS - 1)
        for behind, part in enumerate((t0, t1, t2, t3)):
            source = (rank + MODELS - behind) & (MODELS - 1)
            place = pl.ds(pl.multiple_of(source * rows, rows), rows)
            out[place, :] = jnp.dot(part[...], w[head], preferred_element_type=F32).astype(out.dtype)


def kv_parts(aheads, dtype, rank, parts, weights):
    rows = parts[0].shape[0] * MODELS
    shape = jax.ShapeDtypeStruct((rows, 2 * HEAD_SIZE), dtype)
    return pl.pallas_call(
        functools.partial(kv_parts_kernel, aheads),
        in_specs=[SM] + [VM] * 5,
        out_specs=[VM] * len(aheads),
        out_shape=[shape] * len(aheads),
        compiler_params=params(8),
        cost_estimate=COST,
        name="kv_parts",
    )(rank, *parts, weights)


def q_parts_kernel(rank_ref, t0, t1, t2, t3, wq, *outs):
    rank = rank_ref[0]
    rows = t0.shape[0]
    width = outs[0].shape[1]
    for ahead, out in zip((2, 1, 3, 0), outs):
        column = pl.ds(pl.multiple_of(((rank + ahead) & (MODELS - 1)) * width, width), width)
        for behind, part in enumerate((t0, t1, t2, t3)):
            source = (rank + MODELS - behind) & (MODELS - 1)
            place = pl.ds(pl.multiple_of(source * rows, rows), rows)
            out[place, :] = jnp.dot(part[...], wq[:, column], preferred_element_type=F32).astype(BF)


def q_parts(rank, parts, w_query):
    rows = parts[0].shape[0] * MODELS
    return pl.pallas_call(
        q_parts_kernel,
        in_specs=[SM] + [VM] * 5,
        out_specs=[VM] * MODELS,
        out_shape=[jax.ShapeDtypeStruct((rows, w_query.shape[1] // MODELS), BF)] * MODELS,
        compiler_params=params(8),
        cost_estimate=COST,
        name="query_parts",
    )(rank, *parts, w_query)


def turn(u, cosine, sine):
    return u * cosine + pltpu.roll(u, HEAD_SIZE // 2, 1) * sine


def v_join_kernel(a, b, c, own, out):
    out[...] = (own[...] + a[...].astype(F32) + b[...].astype(F32) + c[...].astype(F32)).astype(BF)


def v_join(a, b, c, own):
    return pl.pallas_call(
        v_join_kernel,
        in_specs=[VM] * 4,
        out_specs=VM,
        out_shape=jax.ShapeDtypeStruct(own.shape, BF),
        compiler_params=params(16),
        cost_estimate=COST,
        name="v_join",
    )(a, b, c, own)


def kv_join_kernel(a, b, c, own, cosine, sine, out):
    total = own[...] + a[...].astype(F32) + b[...].astype(F32) + c[...].astype(F32)
    out[:, :HEAD_SIZE] = turn(total[:, :HEAD_SIZE], cosine[...], sine[...]).astype(BF)
    out[:, HEAD_SIZE:] = total[:, HEAD_SIZE:].astype(BF)


def kv_join(a, b, c, own, cosine, sine):
    return pl.pallas_call(
        kv_join_kernel,
        in_specs=[VM] * 6,
        out_specs=VM,
        out_shape=jax.ShapeDtypeStruct(own.shape, BF),
        compiler_params=params(16),
        cost_estimate=COST,
        name="kv_join",
    )(a, b, c, own, cosine, sine)


def q_join_kernel(a, b, c, d, cosine, sine, out):
    for h in range(out.shape[1] // HEAD_SIZE):
        column = slice(h * HEAD_SIZE, (h + 1) * HEAD_SIZE)
        total = a[:, column].astype(F32) + b[:, column].astype(F32) + c[:, column].astype(F32) + d[:, column].astype(F32)
        out[:, column] = turn(total, cosine[...], sine[...]).astype(BF)


def q_join(a, b, c, d, cosine, sine):
    return pl.pallas_call(
        q_join_kernel,
        in_specs=[VM] * 6,
        out_specs=VM,
        out_shape=jax.ShapeDtypeStruct(a.shape, BF),
        compiler_params=params(8),
        cost_estimate=COST,
        name="q_join",
    )(a, b, c, d, cosine, sine)


def select_kernel(hop, pick_ref, held, *refs):
    more, out = refs[:-1], refs[-1]
    for ahead in range(YS):
        for which in range(CORES):
            out[ahead, which] = held[pick_ref[hop, ahead * CORES + which]]
        for i, one in enumerate(more):
            out[ahead, CORES + i] = one[0]


def select_ends_kernel(near_ref, pick_ref, first, last, out):
    for ahead in range(YS):
        for which in range(CORES):
            at = ahead * CORES + which

            @pl.when(near_ref[ahead] == 1)
            def _():
                out[ahead, which] = first[pick_ref[0, at]]

            @pl.when(near_ref[ahead] == 0)
            def _():
                out[ahead, which] = last[pick_ref[HOPS - 1, at]]


def select(body, scalars, held, extra=0, flops=5000000000):
    return pl.pallas_call(
        body,
        in_specs=[SM] * len(scalars) + [VM] * len(held),
        out_specs=VM,
        out_shape=jax.ShapeDtypeStruct((YS, CORES + extra) + held[0].shape[1:], BF),
        compiler_params=params(4),
        cost_estimate=pl.CostEstimate(flops=flops, bytes_accessed=1, transcendentals=0),
        name="select_blocks",
    )(*scalars, *held)


SIDE = (HOPS - 1) * YS
OWN = 2 * SIDE
SINK = OWN + 4
HELD = SINK + 1
LOG2E = 1.4426950408889634
PAIR = 2


def attend_kernel(index_ref, query, own, sink, *refs):
    near, cross = refs[: HOPS - 2], refs[HOPS - 2 : 2 * (HOPS - 2)]
    last_near, last_cross, out, held, sems = refs[2 * (HOPS - 2) :]
    moves = [(own, OWN, 4), (sink, SINK, 1)]
    for side, given in enumerate((near, cross)):
        for i, one in enumerate(given):
            moves += [(one.at[y, pl.ds(side, 1)], side * SIDE + i * YS + y, 1) for y in range(YS)]
    copies = [pltpu.make_async_copy(a, held.at[pl.ds(at, n)], sems.at[i]) for i, (a, at, n) in enumerate(moves)]
    for copy in copies:
        copy.start()
    for side, one in enumerate((last_near, last_cross)):
        for y in range(YS):
            held[side * SIDE + (HOPS - 2) * YS + y] = one[y, side]
    for copy in copies:
        copy.wait()
    slots = 8
    scale = LOG2E / HEAD_SIZE**0.5
    contract = (((1,), (1,)), ((), ()))
    tall = PAIR * BLOCK
    half = BLOCK // 2

    def score(b, first, places, i):
        rows = slice(b * BLOCK, (b + 1) * BLOCK)
        q = jnp.concatenate(
            [query[rows, (first + h) * HEAD_SIZE : (first + h + 1) * HEAD_SIZE] for h in range(PAIR)], axis=0
        )
        at = jnp.maximum(places[i], 0) if i < slots else OWN + b
        s = lax.dot_general(q, held[at, :, :HEAD_SIZE], contract, preferred_element_type=F32)
        if i < slots:
            return s, jnp.where(places[i] >= 0, jnp.maximum(s[:, :half], s[:, half:]), -jnp.inf)
        row = lax.broadcasted_iota(jnp.int32, (tall, BLOCK), 0) & (BLOCK - 1)
        s = jnp.where(row >= lax.broadcasted_iota(jnp.int32, (tall, BLOCK), 1), s, -jnp.inf)
        return s, jnp.maximum(s[:, :half], s[:, half:])

    def scores(work):
        b, first = work
        places = [index_ref[b * slots + i] for i in range(slots)]
        return [functools.partial(score, b, first, places, i) for i in range(slots + 1)], places

    heads = query.shape[1] // HEAD_SIZE
    works = [(b, first) for b in range(query.shape[0] // BLOCK) for first in range(0, heads, PAIR)]
    calls, places = scores(works[0])
    now = [call() for call in calls]
    for n, (b, first) in enumerate(works):
        calls, later = scores(works[n + 1]) if n + 1 < len(works) else ([], None)
        following = []
        top = functools.reduce(jnp.maximum, [m for _, m in now])
        top = jnp.max(top, axis=1, keepdims=True) * scale
        total = jnp.zeros((tall, half), F32)
        summed = jnp.zeros((tall, HEAD_SIZE), F32)
        for i, (s, _) in enumerate(now):
            if calls:
                following.append(calls[i]())
            at = jnp.maximum(places[i], 0) if i < slots else OWN + b
            shift = jnp.where(places[i] >= 0, top, jnp.inf) if i < slots else top
            weight = jnp.exp2(s * scale - shift)
            total = total + (weight[:, :half] + weight[:, half:])
            summed = summed + jnp.dot(weight.astype(BF), held[at, :, HEAD_SIZE:], preferred_element_type=F32)
        result = (summed / jnp.sum(total, axis=1, keepdims=True)).astype(BF)
        for h in range(PAIR):
            column = slice((first + h) * HEAD_SIZE, (first + h + 1) * HEAD_SIZE)
            out[b * BLOCK : (b + 1) * BLOCK, column] = result[h * BLOCK : (h + 1) * BLOCK]
        now, places = following, later


def attend(index, query, own, sink, near, cross):
    early = [pltpu.with_memory_space_constraint(a, pltpu.HBM) for a in (own, sink, *near[:-1], *cross[:-1])]
    return pl.pallas_call(
        attend_kernel,
        in_specs=[SM, VM] + [HBM] * len(early) + [VM] * 2,
        out_specs=VM,
        out_shape=jax.ShapeDtypeStruct(query.shape, BF),
        scratch_shapes=[
            pltpu.VMEM((HELD, BLOCK, 2 * HEAD_SIZE), BF),
            pltpu.SemaphoreType.DMA((2 + 2 * (HOPS - 2) * YS,)),
        ],
        compiler_params=params(40),
        cost_estimate=COST,
        name="attend",
    )(index, query, *early, near[-1], cross[-1])


def tables(first, rows):
    half = HEAD_SIZE // 2
    position = first + jnp.arange(rows, dtype=jnp.int32)
    freq = THETA ** (-jnp.arange(half, dtype=F32) / half)
    angle = position.astype(F32)[:, None] * freq[None, :]
    cosine, sine = jnp.cos(angle), jnp.sin(angle)
    return jnp.concatenate([cosine, cosine], axis=1), jnp.concatenate([-sine, sine], axis=1)


def picks(listed, z):
    source = ROW * (z - jnp.arange(HOPS, dtype=jnp.int32))[:, None] + jnp.arange(ROW, dtype=jnp.int32)[None, :]
    flat = listed.reshape(-1)
    named = (flat[None, None, :] >= 1) & ((flat >> 2)[None, None, :] == source[:, :, None])
    return jnp.max(jnp.where(named, flat & 3, 0), axis=-1)


def on_device(tokens, w_query, key_weight, value_weight, block_list):
    seq = lax.axis_index("seq").astype(jnp.int32)
    rank_ref = lax.axis_index("mdl").astype(jnp.int32).reshape(1)
    rows = tokens.shape[0] * MODELS
    part2, part1, part3 = split((2, 1, 3), rank_ref, tokens)
    part2, part1, part3, seq, block_list = lax.optimization_barrier((part2, part1, part3, seq, block_list))
    part2 = along_x(part2, 2)
    part1 = along_x(part1, 1)
    part3 = along_x(part3, 3)
    [part0] = split((0,), rank_ref, tokens)
    parts = (part0, part1, part2, part3)

    z, y, core = seq >> 3, (seq >> 1) & 3, seq & 1
    mine = picks(block_list, z)
    both = jnp.stack([mine, other_core(mine)])
    wanted = exchange_y(jnp.broadcast_to(both[None], (YS,) + both.shape))
    pick = lax.dynamic_index_in_dim(wanted, y * CORES + core, 3, keepdims=False)
    pick = jnp.transpose(pick, (2, 0, 1)).reshape(HOPS, YS * CORES)
    ahead = jnp.arange(YS, dtype=jnp.int32)
    near_first = ((ahead > y) | ((ahead == y) & (core == 0))).astype(jnp.int32)

    source = block_list >> 2
    hop = z - (source >> 3)
    cross = (source & 1) ^ core
    index = cross * SIDE + jnp.where(hop == 0, HOPS - 2, hop - 1) * YS + ((source >> 1) & 3)
    index = jnp.where(source == seq, OWN + (block_list & 3), index)
    index = jnp.where(block_list == 0, SINK, index)
    index = jnp.where(block_list < 0, -1, index).reshape(-1)

    cosine, sine = tables(seq * rows, rows)
    weights = join_weights(key_weight, value_weight)
    parts, pick, near_first, cosine, sine, index, weights = lax.optimization_barrier(
        (parts, pick, near_first, cosine, sine, index, weights)
    )

    kv2, kv1, kv3 = kv_parts((2, 1, 3), BF, rank_ref, parts, weights)
    parts, kv2 = lax.optimization_barrier((parts, kv2))
    kv2 = along_x(kv2, 2)
    kv1 = along_x(kv1, 1)
    kv3 = along_x(kv3, 3)
    q2, q1, q3, q0 = q_parts(rank_ref, parts, w_query)
    parts, q2 = lax.optimization_barrier((parts, q2))
    [kv0] = kv_parts((0,), F32, rank_ref, parts, weights)
    own = kv_join(kv1, kv2, kv3, kv0, cosine, sine).reshape(4, BLOCK, 2 * HEAD_SIZE)

    own, q2 = lax.optimization_barrier((own, q2))
    q2 = along_x(q2, 2)

    over = lax.ppermute(own[:1], "seq", [(0, 1)])
    held = along_z(own, 1)
    near = []
    for hop in range(1, HOPS - 1):
        onward = along_z(held, 1)
        if hop == 1:
            sent = select(
                functools.partial(select_kernel, hop), [pick], [held, jnp.where(core == 0, own[:1], over)], 1
            )
        else:
            sent = select(
                functools.partial(select_kernel, hop), [pick], [held], flops=10000000000 if hop == 2 else 5000000000
            )
            sent, near[-1] = lax.optimization_barrier((sent, near[-1]))
        if hop == 2:
            sink = near[0][0, CORES:]
            got = along_rows(sink, (0,), 4)
            onward, q2, q1, q3 = lax.optimization_barrier((onward, q2, q1, q3))
            q1 = along_x(q1, 1)
            q3 = along_x(q3, 3)
        if hop == 3:
            sent, got = lax.optimization_barrier((sent, got))
            sink = jnp.where(z == 4, got, sink)
            got = along_rows(sink, (0, 4), 2)
        near.append(exchange_y(sent))
        held = onward
    sent = select(select_ends_kernel, [near_first, pick], [own, held])
    sent, near[-1], got = lax.optimization_barrier((sent, near[-1], got))
    sink = jnp.where((z == 2) | (z == 6), got, sink)
    got = along_rows(sink, (0, 2, 4, 6), 1)
    sink = jnp.where((z & 1) == 1, got, sink)
    near.append(exchange_y(sent))
    query = q_join(q0, q1, q2, q3, cosine, sine)
    near[-1], query, sink = lax.optimization_barrier((near[-1], query, sink))
    across = [other_core(one) for one in near]
    return attend(index, query, own, sink, near, across)


def solution(mesh):
    in_specs = (
        P(("seq", "mdl"), None),
        P("mdl", None),
        P("mdl", None),
        P("mdl", None),
        P("seq", None),
    )
    return jax.shard_map(
        on_device, mesh=mesh, in_specs=in_specs, out_specs=P("seq", "mdl"), check_vma=False
    )
```

```python
import functools

import jax
import jax.numpy as jnp
from jax import lax
from jax.experimental import pallas as pl
from jax.experimental.pallas import tpu as pltpu
from jax.sharding import PartitionSpec as P

HEAD_SIZE = 128
BLOCK = 256
THETA = 1000000.0
CORES = 2
YS = 4
ROW = CORES * YS
HOPS = 5
MODELS = 4
FAR = HOPS * YS * CORES
VM = pl.BlockSpec(memory_space=pltpu.VMEM)
SM = pl.BlockSpec(memory_space=pltpu.SMEM)
HBM = pl.BlockSpec(memory_space=pltpu.HBM)
BF = jnp.bfloat16
F32 = jnp.float32


COST = pl.CostEstimate(flops=1, bytes_accessed=1, transcendentals=0)


def params(mib):
    return pltpu.CompilerParams(vmem_limit_bytes=mib * 2**20)


def along_x(value, steps):
    return lax.ppermute(value, "mdl", [(i, (i + steps) % MODELS) for i in range(MODELS)])


def along_z(value, steps):
    count = lax.axis_size("seq")
    return lax.ppermute(value, "seq", [(i, i + ROW * steps) for i in range(count - ROW * steps)])


def along_rows(value, rows, steps):
    pairs = [(i * ROW + j, (i + steps) * ROW + j) for i in rows for j in range(ROW)]
    return lax.ppermute(value, "seq", pairs)


def exchange_y(value):
    count = lax.axis_size("seq")
    groups = [
        [first + y * CORES + c for y in range(YS)] for first in range(0, count, ROW) for c in range(CORES)
    ]
    return lax.all_to_all(value, "seq", split_axis=0, concat_axis=0, axis_index_groups=groups)


def other_core(value):
    count = lax.axis_size("seq")
    return lax.ppermute(value, "seq", [(i, i ^ 1) for i in range(count)])


def columns_of(rank_ref, ahead, width):
    return pl.ds(pl.multiple_of(((rank_ref[0] + ahead) & (MODELS - 1)) * width, width), width)


def split_kernel(aheads, rank_ref, tokens, *refs):
    outs, sems = refs[:-1], refs[-1]
    width = outs[0].shape[1]
    copies = [
        pltpu.make_async_copy(tokens.at[:, columns_of(rank_ref, ahead, width)], outs[i], sems.at[i])
        for i, ahead in enumerate(aheads)
    ]
    for copy in copies:
        copy.start()
    for copy in copies:
        copy.wait()


def split(aheads, rank, tokens):
    shape = jax.ShapeDtypeStruct((tokens.shape[0], tokens.shape[1] // MODELS), BF)
    return pl.pallas_call(
        functools.partial(split_kernel, aheads),
        in_specs=[SM, HBM],
        out_specs=[VM] * len(aheads),
        out_shape=[shape] * len(aheads),
        scratch_shapes=[pltpu.SemaphoreType.DMA((len(aheads),))],
        compiler_params=params(4),
        cost_estimate=COST,
        name="split_columns",
    )(rank, pltpu.with_memory_space_constraint(tokens, pltpu.HBM))


def join_weights_kernel(wk, wv, out):
    for head in range(MODELS):
        column = slice(head * HEAD_SIZE, (head + 1) * HEAD_SIZE)
        out[head, :, :HEAD_SIZE] = wk[:, column]
        out[head, :, HEAD_SIZE:] = wv[:, column]


def join_weights(key_weight, value_weight):
    return pl.pallas_call(
        join_weights_kernel,
        in_specs=[VM] * 2,
        out_specs=VM,
        out_shape=jax.ShapeDtypeStruct((MODELS, key_weight.shape[0], 2 * HEAD_SIZE), BF),
        compiler_params=params(4),
        cost_estimate=COST,
        name="join_weights",
    )(key_weight, value_weight)


def kv_parts_kernel(aheads, rank_ref, t0, t1, t2, t3, w, *outs):
    rank = rank_ref[0]
    rows = t0.shape[0]
    for ahead, out in zip(aheads, outs):
        head = (rank + ahead) & (MODELS - 1)
        for behind, part in enumerate((t0, t1, t2, t3)):
            source = (rank + MODELS - behind) & (MODELS - 1)
            place = pl.ds(pl.multiple_of(source * rows, rows), rows)
            out[place, :] = jnp.dot(part[...], w[head], preferred_element_type=F32).astype(out.dtype)


def kv_parts(aheads, dtype, rank, parts, weights):
    rows = parts[0].shape[0] * MODELS
    shape = jax.ShapeDtypeStruct((rows, 2 * HEAD_SIZE), dtype)
    return pl.pallas_call(
        functools.partial(kv_parts_kernel, aheads),
        in_specs=[SM] + [VM] * 5,
        out_specs=[VM] * len(aheads),
        out_shape=[shape] * len(aheads),
        compiler_params=params(8),
        cost_estimate=COST,
        name="kv_parts",
    )(rank, *parts, weights)


def q_parts_kernel(rank_ref, t0, t1, t2, t3, wq, *outs):
    rank = rank_ref[0]
    rows = t0.shape[0]
    width = outs[0].shape[1]
    for ahead, out in zip((2, 1, 3, 0), outs):
        column = pl.ds(pl.multiple_of(((rank + ahead) & (MODELS - 1)) * width, width), width)
        for behind, part in enumerate((t0, t1, t2, t3)):
            source = (rank + MODELS - behind) & (MODELS - 1)
            place = pl.ds(pl.multiple_of(source * rows, rows), rows)
            out[place, :] = jnp.dot(part[...], wq[:, column], preferred_element_type=F32).astype(BF)


def q_parts(rank, parts, w_query):
    rows = parts[0].shape[0] * MODELS
    return pl.pallas_call(
        q_parts_kernel,
        in_specs=[SM] + [VM] * 5,
        out_specs=[VM] * MODELS,
        out_shape=[jax.ShapeDtypeStruct((rows, w_query.shape[1] // MODELS), BF)] * MODELS,
        compiler_params=params(8),
        cost_estimate=COST,
        name="query_parts",
    )(rank, *parts, w_query)


def turn(u, cosine, sine):
    return u * cosine + pltpu.roll(u, HEAD_SIZE // 2, 1) * sine


def v_join_kernel(a, b, c, own, out):
    out[...] = (own[...] + a[...].astype(F32) + b[...].astype(F32) + c[...].astype(F32)).astype(BF)


def v_join(a, b, c, own):
    return pl.pallas_call(
        v_join_kernel,
        in_specs=[VM] * 4,
        out_specs=VM,
        out_shape=jax.ShapeDtypeStruct(own.shape, BF),
        compiler_params=params(16),
        cost_estimate=COST,
        name="v_join",
    )(a, b, c, own)


def kv_join_kernel(a, b, c, own, cosine, sine, out):
    total = own[...] + a[...].astype(F32) + b[...].astype(F32) + c[...].astype(F32)
    out[:, :HEAD_SIZE] = turn(total[:, :HEAD_SIZE], cosine[...], sine[...]).astype(BF)
    out[:, HEAD_SIZE:] = total[:, HEAD_SIZE:].astype(BF)


def kv_join(a, b, c, own, cosine, sine):
    return pl.pallas_call(
        kv_join_kernel,
        in_specs=[VM] * 6,
        out_specs=VM,
        out_shape=jax.ShapeDtypeStruct(own.shape, BF),
        compiler_params=params(16),
        cost_estimate=COST,
        name="kv_join",
    )(a, b, c, own, cosine, sine)


def q_join_kernel(a, b, c, d, cosine, sine, out):
    for h in range(out.shape[1] // HEAD_SIZE):
        column = slice(h * HEAD_SIZE, (h + 1) * HEAD_SIZE)
        total = a[:, column].astype(F32) + b[:, column].astype(F32) + c[:, column].astype(F32) + d[:, column].astype(F32)
        out[:, column] = turn(total, cosine[...], sine[...]).astype(BF)


def q_join(a, b, c, d, cosine, sine):
    return pl.pallas_call(
        q_join_kernel,
        in_specs=[VM] * 6,
        out_specs=VM,
        out_shape=jax.ShapeDtypeStruct(a.shape, BF),
        compiler_params=params(8),
        cost_estimate=COST,
        name="q_join",
    )(a, b, c, d, cosine, sine)


def select_kernel(hop, pick_ref, held, out):
    for ahead in range(YS):
        for which in range(CORES):
            out[ahead, which] = held[pick_ref[hop, ahead * CORES + which]]


def select_ends_kernel(near_ref, pick_ref, first, last, out):
    for ahead in range(YS):
        for which in range(CORES):
            at = ahead * CORES + which

            @pl.when(near_ref[ahead] == 1)
            def _():
                out[ahead, which] = first[pick_ref[0, at]]

            @pl.when(near_ref[ahead] == 0)
            def _():
                out[ahead, which] = last[pick_ref[HOPS - 1, at]]


def select(body, scalars, held, flops=5000000000):
    return pl.pallas_call(
        body,
        in_specs=[SM] * len(scalars) + [VM] * len(held),
        out_specs=VM,
        out_shape=jax.ShapeDtypeStruct((YS, CORES) + held[0].shape[1:], BF),
        compiler_params=params(4),
        cost_estimate=pl.CostEstimate(flops=flops, bytes_accessed=1, transcendentals=0),
        name="select_blocks",
    )(*scalars, *held)


SIDE = (HOPS - 1) * YS
OWN = 2 * SIDE
SINK = OWN + 4
HELD = SINK + 1
LOG2E = 1.4426950408889634
PAIR = 2


def attend_kernel(index_ref, query, own, sink, *refs):
    near, cross = refs[: HOPS - 2], refs[HOPS - 2 : 2 * (HOPS - 2)]
    last_near, last_cross, out, held, sems = refs[2 * (HOPS - 2) :]
    moves = [(own, OWN, 4), (sink, SINK, 1)]
    for side, given in enumerate((near, cross)):
        for i, one in enumerate(given):
            moves += [(one.at[y, pl.ds(side, 1)], side * SIDE + i * YS + y, 1) for y in range(YS)]
    copies = [pltpu.make_async_copy(a, held.at[pl.ds(at, n)], sems.at[i]) for i, (a, at, n) in enumerate(moves)]
    for copy in copies:
        copy.start()
    for side, one in enumerate((last_near, last_cross)):
        for y in range(YS):
            held[side * SIDE + (HOPS - 2) * YS + y] = one[y, side]
    for copy in copies:
        copy.wait()
    slots = 8
    scale = LOG2E / HEAD_SIZE**0.5
    contract = (((1,), (1,)), ((), ()))
    tall = PAIR * BLOCK
    half = BLOCK // 2

    def score(b, first, places, i):
        rows = slice(b * BLOCK, (b + 1) * BLOCK)
        q = jnp.concatenate(
            [query[rows, (first + h) * HEAD_SIZE : (first + h + 1) * HEAD_SIZE] for h in range(PAIR)], axis=0
        )
        at = jnp.maximum(places[i], 0) if i < slots else OWN + b
        s = lax.dot_general(q, held[at, :, :HEAD_SIZE], contract, preferred_element_type=F32)
        if i < slots:
            return s, jnp.where(places[i] >= 0, jnp.maximum(s[:, :half], s[:, half:]), -jnp.inf)
        row = lax.broadcasted_iota(jnp.int32, (tall, BLOCK), 0) & (BLOCK - 1)
        s = jnp.where(row >= lax.broadcasted_iota(jnp.int32, (tall, BLOCK), 1), s, -jnp.inf)
        return s, jnp.maximum(s[:, :half], s[:, half:])

    def scores(work):
        b, first = work
        places = [index_ref[b * slots + i] for i in range(slots)]
        return [functools.partial(score, b, first, places, i) for i in range(slots + 1)], places

    heads = query.shape[1] // HEAD_SIZE
    works = [(b, first) for b in range(query.shape[0] // BLOCK) for first in range(0, heads, PAIR)]
    calls, places = scores(works[0])
    now = [call() for call in calls]
    for n, (b, first) in enumerate(works):
        calls, later = scores(works[n + 1]) if n + 1 < len(works) else ([], None)
        following = []
        top = functools.reduce(jnp.maximum, [m for _, m in now])
        top = jnp.max(top, axis=1, keepdims=True) * scale
        total = jnp.zeros((tall, half), F32)
        summed = jnp.zeros((tall, HEAD_SIZE), F32)
        for i, (s, _) in enumerate(now):
            if calls:
                following.append(calls[i]())
            at = jnp.maximum(places[i], 0) if i < slots else OWN + b
            shift = jnp.where(places[i] >= 0, top, jnp.inf) if i < slots else top
            weight = jnp.exp2(s * scale - shift)
            total = total + (weight[:, :half] + weight[:, half:])
            summed = summed + jnp.dot(weight.astype(BF), held[at, :, HEAD_SIZE:], preferred_element_type=F32)
        result = (summed / jnp.sum(total, axis=1, keepdims=True)).astype(BF)
        for h in range(PAIR):
            column = slice((first + h) * HEAD_SIZE, (first + h + 1) * HEAD_SIZE)
            out[b * BLOCK : (b + 1) * BLOCK, column] = result[h * BLOCK : (h + 1) * BLOCK]
        now, places = following, later


def attend(index, query, own, sink, near, cross):
    early = [pltpu.with_memory_space_constraint(a, pltpu.HBM) for a in (own, sink, *near[:-1], *cross[:-1])]
    return pl.pallas_call(
        attend_kernel,
        in_specs=[SM, VM] + [HBM] * len(early) + [VM] * 2,
        out_specs=VM,
        out_shape=jax.ShapeDtypeStruct(query.shape, BF),
        scratch_shapes=[
            pltpu.VMEM((HELD, BLOCK, 2 * HEAD_SIZE), BF),
            pltpu.SemaphoreType.DMA((2 + 2 * (HOPS - 2) * YS,)),
        ],
        compiler_params=params(40),
        cost_estimate=COST,
        name="attend",
    )(index, query, *early, near[-1], cross[-1])


def tables(first, rows):
    half = HEAD_SIZE // 2
    position = first + jnp.arange(rows, dtype=jnp.int32)
    freq = THETA ** (-jnp.arange(half, dtype=F32) / half)
    angle = position.astype(F32)[:, None] * freq[None, :]
    cosine, sine = jnp.cos(angle), jnp.sin(angle)
    return jnp.concatenate([cosine, cosine], axis=1), jnp.concatenate([-sine, sine], axis=1)


def picks(listed, z):
    source = ROW * (z - jnp.arange(HOPS, dtype=jnp.int32))[:, None] + jnp.arange(ROW, dtype=jnp.int32)[None, :]
    flat = listed.reshape(-1)
    named = (flat[None, None, :] >= 1) & ((flat >> 2)[None, None, :] == source[:, :, None])
    return jnp.max(jnp.where(named, flat & 3, 0), axis=-1)


def on_device(tokens, w_query, key_weight, value_weight, block_list):
    seq = lax.axis_index("seq").astype(jnp.int32)
    rank_ref = lax.axis_index("mdl").astype(jnp.int32).reshape(1)
    rows = tokens.shape[0] * MODELS
    part2, part1, part3 = split((2, 1, 3), rank_ref, tokens)
    part2, part1, part3, seq, block_list = lax.optimization_barrier((part2, part1, part3, seq, block_list))
    part2 = along_x(part2, 2)
    part1 = along_x(part1, 1)
    part3 = along_x(part3, 3)
    [part0] = split((0,), rank_ref, tokens)
    parts = (part0, part1, part2, part3)

    z, y, core = seq >> 3, (seq >> 1) & 3, seq & 1
    mine = picks(block_list, z)
    both = jnp.stack([mine, other_core(mine)])
    wanted = exchange_y(jnp.broadcast_to(both[None], (YS,) + both.shape))
    pick = lax.dynamic_index_in_dim(wanted, y * CORES + core, 3, keepdims=False)
    pick = jnp.transpose(pick, (2, 0, 1)).reshape(HOPS, YS * CORES)
    ahead = jnp.arange(YS, dtype=jnp.int32)
    near_first = ((ahead > y) | ((ahead == y) & (core == 0))).astype(jnp.int32)

    source = block_list >> 2
    hop = z - (source >> 3)
    cross = (source & 1) ^ core
    index = cross * SIDE + jnp.where(hop == 0, HOPS - 2, hop - 1) * YS + ((source >> 1) & 3)
    index = jnp.where(source == seq, OWN + (block_list & 3), index)
    index = jnp.where(block_list == 0, SINK, index)
    index = jnp.where(block_list < 0, -1, index).reshape(-1)

    cosine, sine = tables(seq * rows, rows)
    weights = join_weights(key_weight, value_weight)
    parts, pick, near_first, cosine, sine, index, weights = lax.optimization_barrier(
        (parts, pick, near_first, cosine, sine, index, weights)
    )

    kv2, kv1, kv3 = kv_parts((2, 1, 3), BF, rank_ref, parts, weights)
    parts, kv2 = lax.optimization_barrier((parts, kv2))
    kv2 = along_x(kv2, 2)
    kv1 = along_x(kv1, 1)
    kv3 = along_x(kv3, 3)
    q2, q1, q3, q0 = q_parts(rank_ref, parts, w_query)
    parts, q2 = lax.optimization_barrier((parts, q2))
    [kv0] = kv_parts((0,), F32, rank_ref, parts, weights)
    own = kv_join(kv1, kv2, kv3, kv0, cosine, sine).reshape(4, BLOCK, 2 * HEAD_SIZE)

    own, q2 = lax.optimization_barrier((own, q2))
    q2 = along_x(q2, 2)

    held = along_z(own, 1)
    sink = jnp.where(core == 0, own[:1], lax.ppermute(own[:1], "seq", [(0, 1)]))
    along_y = [lax.ppermute(sink, "seq", [(c, to * CORES + c) for c in range(CORES)]) for to in range(1, YS)]
    near = []
    for hop in range(1, HOPS - 1):
        onward = along_z(held, 1)
        sent = select(
            functools.partial(select_kernel, hop), [pick], [held], flops=10000000000 if hop == 2 else 5000000000
        )
        if hop > 1:
            sent, near[-1] = lax.optimization_barrier((sent, near[-1]))
        if hop == 2:
            sent, along_y = lax.optimization_barrier((sent, along_y))
            for to, one in enumerate(along_y, 1):
                sink = jnp.where(y == to, one, sink)
            got = along_rows(sink, (0,), 4)
            onward, q2, q1, q3 = lax.optimization_barrier((onward, q2, q1, q3))
            q1 = along_x(q1, 1)
            q3 = along_x(q3, 3)
        if hop == 3:
            sent, got = lax.optimization_barrier((sent, got))
            sink = jnp.where(z == 4, got, sink)
            got = along_rows(sink, (0, 4), 2)
        near.append(exchange_y(sent))
        held = onward
    sent = select(select_ends_kernel, [near_first, pick], [own, held])
    sent, near[-1], got, q1, q3 = lax.optimization_barrier((sent, near[-1], got, q1, q3))
    sink = jnp.where((z == 2) | (z == 6), got, sink)
    got = along_rows(sink, (0, 2, 4, 6), 1)
    sink = jnp.where((z & 1) == 1, got, sink)
    near.append(exchange_y(sent))
    query = q_join(q0, q1, q2, q3, cosine, sine)
    near[-1], query, sink = lax.optimization_barrier((near[-1], query, sink))
    across = [other_core(one) for one in near]
    return attend(index, query, own, sink, near, across)


def solution(mesh):
    in_specs = (
        P(("seq", "mdl"), None),
        P("mdl", None),
        P("mdl", None),
        P("mdl", None),
        P("seq", None),
    )
    return jax.shard_map(
        on_device, mesh=mesh, in_specs=in_specs, out_specs=P("seq", "mdl"), check_vma=False
    )
```
